32 devices in a mesh: section: 4 (over x, core), shard: 8 (over z, y).
Axes of the slice: x: 2, y: 2, z: 4, core: 2. Of those that a mesh axis runs over, the one named last changes fastest.
Arguments:
- hidden: bfloat16 [256, 8192], P(('section', 'shard')), may hold values from -6 to 6
- norm_gain: float32 [4, 8192], P('section'), may hold values from 0.1 to 1.9
- gate_weight: bfloat16 [4, 8192, 16384], P('section', None, 'shard'), may hold values from -0.0625 to 0.0625
- up_weight: bfloat16 [4, 8192, 16384], P('section', None, 'shard'), may hold values from -0.0625 to 0.0625
- head_vector: bfloat16 [4, 16384], P('section', 'shard'), may hold values from -0.046875 to 0.046875
- pack_slot: int32 [4, 256], replicated, may hold values from 0 to 255, each once within a row
- owner_slot: int32 [256], replicated, may hold values from 0 to 255, each once
Outputs:
- section_scores: float32 [4, 256], P('section', 'shard')
- joined: float32 [4, 256], P(None, ('section', 'shard'))
The draws below stay inside these ranges and needn't reach their ends.
All inputs are finite; a program needn't handle non-finite values.
Results may differ from the reference program's by a relative error of at most 0.0032.
Values may be sent and summed in bfloat16 or wider, within the bound.
A program may use at most 128 MiB of HBM per device.

```python
import jax
import jax.numpy as jnp
from jax import lax

D = 8192
FFW = 16384
ROWS = 256


def block_scale(key, dims, shards, least, largest):
    level, own = 1.0, jax.random.fold_in(key, 6)
    for axis_at, blocks in shards:
        heights = jnp.exp(jax.random.uniform(jax.random.fold_in(own, axis_at), (blocks,), jnp.float32, least / len(shards), largest / len(shards)))
        level = level * jnp.repeat(heights, dims[axis_at] // blocks).reshape([-1 if axis == axis_at else 1 for axis in range(len(dims))])
    return level


def scatter_about(rng, shape, deviation, reach, pieces=(), dtype=jnp.bfloat16):
    factor_of = block_scale(rng, shape, pieces, -0.22, 0.18) if pieces else 1.0
    entries = jax.random.normal(rng, shape, jnp.float32) * deviation * factor_of
    return jnp.minimum(jnp.maximum(entries, -reach), reach).astype(dtype)


def setup_inputs(seed: int = 0) -> dict:
    streams_of = jax.random.split(jax.random.key(seed), 8)
    return {
        "hidden": scatter_about(streams_of[0], (ROWS, D), 1.0, 6.0, ((0, 32),)),
        "norm_gain": jnp.clip(1.0 + 0.18 * jax.random.normal(streams_of[1], (4, D), jnp.float32), 0.1, 1.9),
        "gate_weight": scatter_about(streams_of[2], (4, D, FFW), D ** -0.5, 0.0625, ((0, 4), (2, 8))),
        "up_weight": scatter_about(streams_of[3], (4, D, FFW), D ** -0.5, 0.0625, ((0, 4), (2, 8))),
        "head_vector": scatter_about(streams_of[4], (4, FFW), FFW ** -0.5, 0.046875, ((0, 4), (1, 8))),
        "pack_slot": jax.vmap(lambda own: jax.random.permutation(own, ROWS))(jax.random.split(streams_of[5], 4)).reshape((4, ROWS)).astype(jnp.int32),
        "owner_slot": jax.random.permutation(streams_of[6], ROWS).astype(jnp.int32),
    }


epsilon = 1e-06

def reference(hidden, norm_gain, gate_weight, up_weight, head_vector, pack_slot, owner_slot):
    widened = hidden.astype(jnp.float32)
    inv_rms = lax.rsqrt(lax.optimization_barrier(jnp.mean(widened * widened, axis=1, keepdims=True)) + epsilon)
    section_outputs = []
    joined = jnp.zeros((4, ROWS), jnp.float32)
    for section in range(4):
        normed = (widened * inv_rms * norm_gain[section]).astype(jnp.bfloat16)
        gate_out = jnp.dot(normed, gate_weight[section], preferred_element_type=jnp.float32)
        up_out = jnp.dot(normed, up_weight[section], preferred_element_type=jnp.float32)
        activated = jax.nn.silu(gate_out) * up_out
        scores = jnp.dot(activated, head_vector[section].astype(jnp.float32), precision=lax.Precision.HIGHEST)
        if section == 1 or section == 3:
            scores = jax.nn.log_sigmoid(scores)
        packed = jnp.zeros((ROWS,), jnp.float32).at[pack_slot[section]].set(scores)
        section_outputs.append(packed)
        joined = joined.at[section, owner_slot].set(scores)
    return (jnp.stack(section_outputs), joined)
```

```python
import functools

import jax
import jax.numpy as jnp
from jax import lax
from jax.experimental import pallas as pl
from jax.experimental.pallas import tpu as pltpu
from jax.sharding import PartitionSpec as P

epsilon = 1e-06
MESH = pl.DeviceIdType.MESH
CHUNKS = 16
COLUMN_TILE = 512
ROW_TILE = 256
LANES = 128
VMEM_BUDGET = 58 * 2**20


def kernel(
    sections, shards, slots,
    hidden_ref, gain_ref, head_ref, pack_ref, owner_ref, gate_ref, up_ref,
    scores_ref, joined_ref,
    rows_buf, inv_buf, gate_ring, up_ring, normed, gate_acc, up_acc, part,
    pack_col, owner_col, message, partials, join_out, join_in,
    ring_sem, line_send, line_recv, z_send, z_recv, sum_send, sum_recv, join_send, join_recv,
):
    chunks, _, depth_z, _, _, half = rows_buf.shape
    width = 2 * half
    total_rows = pack_ref.shape[1]
    own_units = head_ref.shape[1]
    section_rows = total_rows // sections

    section = lax.axis_index("section")
    shard = lax.axis_index("shard")
    x, core = section // 2, section % 2
    z, y = shard // 2, shard % 2
    across_x = (section + 2) % sections
    across_core = 2 * x + 1 - core
    across_y = 1 - y
    shard_y = 2 * z + across_y

    def weight_copies(q):
        slot = q % slots
        rows = pl.ds(pl.multiple_of(q * width, width), width)
        return (
            pltpu.make_async_copy(gate_ref.at[0, rows, :], gate_ring.at[slot], ring_sem.at[slot, 0]),
            pltpu.make_async_copy(up_ref.at[0, rows, :], up_ring.at[slot], ring_sem.at[slot, 1]),
        )

    def load_weights(q):
        for copy in weight_copies(q):
            copy.start()

    pl.loop(0, slots)(load_weights)

    barrier = pltpu.get_barrier_semaphore()
    for step in range(1, shards):
        pl.semaphore_signal(barrier, inc=1, device_id=(section, (shard + step) % shards), device_id_type=MESH)
    for step in range(1, sections):
        pl.semaphore_signal(barrier, inc=1, device_id=((section + step) % sections, shard), device_id_type=MESH)

    widened = hidden_ref[...].astype(jnp.float32)
    inv = lax.rsqrt(jnp.mean(widened * widened, axis=1, keepdims=True) + epsilon)
    inv_buf[section, z, y] = jnp.broadcast_to(inv, inv_buf.shape[3:])
    for q in range(chunks):
        low = widened[:, q * width : q * width + half]
        high = widened[:, q * width + half : (q + 1) * width]
        rows_buf[q, section, z, y] = jnp.concatenate([low, high], axis=0).astype(jnp.bfloat16)

    pl.semaphore_wait(barrier, shards - 1 + sections - 1)

    def line(q, sec, row):
        return inv_buf.at[sec, :, row] if q is None else rows_buf.at[q, sec, :, row]

    def sem_row(q):
        return chunks if q is None else q

    def z_copy(q, step):
        block = inv_buf.at[section, z, y] if q is None else rows_buf.at[q, section, z, y]
        at = sem_row(q)
        return pltpu.make_async_remote_copy(
            src_ref=block, dst_ref=block,
            send_sem=z_send.at[at, step], recv_sem=z_recv.at[at, step],
            device_id=(section, 2 * ((z + step) % depth_z) + y), device_id_type=MESH,
        )

    def line_copy(q, kind):
        if kind == 0:
            source, target = (section, y), (across_x, shard)
        elif kind == 1:
            source, target = (section, y), (section, shard_y)
        elif kind == 2:
            odd = 0 if q is None else q % 2
            source = (across_x + odd * (section - across_x), y + odd * (across_y - y))
            target = (section + odd * (across_x - section), shard_y + odd * (shard - shard_y))
        else:
            source = ((section, y), (across_x, y), (section, across_y), (across_x, across_y))[kind - 3]
            target = (across_core, shard)
        part_line = line(q, *source)
        at = sem_row(q)
        return pltpu.make_async_remote_copy(
            src_ref=part_line, dst_ref=part_line,
            send_sem=line_send.at[at, kind], recv_sem=line_recv.at[at, kind],
            device_id=target, device_id_type=MESH,
        )

    def send_z(q):
        for step in range(1, depth_z):
            z_copy(q, step).start()

    def send_line(q):
        for step in range(1, depth_z):
            z_copy(q, step).wait_recv()
        for kind in (0, 1, 3):
            line_copy(q, kind).start()

    def forward_line(q):
        line_copy(q, 0).wait_recv()
        line_copy(q, 1).wait_recv()
        for kind in (2, 4, 5):
            line_copy(q, kind).start()

    def forward_diagonal(q):
        line_copy(q, 2).wait_recv()
        line_copy(q, 6).start()

    def collect(q):
        for kind in (3, 4, 5, 6):
            line_copy(q, kind).wait_recv()

    send_z(None)
    pl.loop(0, chunks)(send_z)

    sub = lax.broadcasted_iota(jnp.int32, (total_rows, total_rows), 0)
    lane = lax.broadcasted_iota(jnp.int32, (total_rows, total_rows), 1)
    pack_row = pack_ref[pl.ds(section, 1), :]
    pack_col[...] = jnp.sum(jnp.where(sub == lane, pack_row, 0), axis=1, keepdims=True)
    owner_col[...] = jnp.sum(jnp.where(sub == lane, owner_ref[...], 0), axis=1, keepdims=True)

    row_tiles = total_rows // ROW_TILE
    column_tiles = own_units // COLUMN_TILE

    def tile(index):
        rows = pl.ds(pl.multiple_of((index // column_tiles) * ROW_TILE, ROW_TILE), ROW_TILE)
        columns = pl.ds(pl.multiple_of((index % column_tiles) * COLUMN_TILE, COLUMN_TILE), COLUMN_TILE)
        return rows, columns

    @pl.loop(0, row_tiles * column_tiles)
    def _(index):
        at = tile(index)
        gate_acc[at] = jnp.zeros((ROW_TILE, COLUMN_TILE), jnp.float32)
        up_acc[at] = jnp.zeros((ROW_TILE, COLUMN_TILE), jnp.float32)

    part[...] = jnp.zeros_like(part)

    def compute(q):
        for sec in range(sections):
            rows = slice(sec * section_rows, (sec + 1) * section_rows)
            inv_rows = inv_buf[sec].reshape(section_rows, LANES)[:, :1]
            stacked = rows_buf[q, sec].astype(jnp.float32)
            for side in range(2):
                columns = pl.ds(pl.multiple_of(q * width + side * half, half), half)
                values = stacked[:, :, side * 8 : side * 8 + 8, :].reshape(section_rows, half)
                scaled = values * inv_rows * gain_ref[:, columns]
                normed[rows, side * half : (side + 1) * half] = scaled.astype(jnp.bfloat16)
        for copy in weight_copies(q):
            copy.wait()
        slot = q % slots

        @pl.loop(0, row_tiles * column_tiles)
        def _(index):
            rows, columns = tile(index)
            left = normed[rows, :]
            gate_acc[rows, columns] += jnp.dot(left, gate_ring[slot, :, columns], preferred_element_type=jnp.float32)
            up_acc[rows, columns] += jnp.dot(left, up_ring[slot, :, columns], preferred_element_type=jnp.float32)

        @pl.when(q + slots < chunks)
        def _():
            load_weights(q + slots)

    @pl.loop(0, chunks + 3)
    def _(t):
        @pl.when(t == 0)
        def _():
            send_line(None)

        @pl.when(t < chunks)
        def _():
            send_line(t)

        @pl.when(t == 1)
        def _():
            forward_line(None)

        @pl.when(jnp.logical_and(t >= 1, t < chunks + 1))
        def _():
            forward_line(t - 1)

        @pl.when(t == 2)
        def _():
            forward_diagonal(None)

        @pl.when(jnp.logical_and(t >= 2, t < chunks + 2))
        def _():
            forward_diagonal(t - 2)

        @pl.when(t == 3)
        def _():
            collect(None)

        @pl.when(t >= 3)
        def _():
            collect(t - 3)
            compute(t - 3)

    @pl.loop(0, row_tiles * (own_units // LANES))
    def _(index):
        per_row = own_units // LANES
        rows = pl.ds(pl.multiple_of((index // per_row) * ROW_TILE, ROW_TILE), ROW_TILE)
        columns = pl.ds(pl.multiple_of((index % per_row) * LANES, LANES), LANES)
        gate = gate_acc[rows, columns]
        activated = gate / (1.0 + jnp.exp(-gate)) * up_acc[rows, columns]
        part[rows, :] += activated * head_ref[:, columns].astype(jnp.float32)

    own_col = jnp.sum(part[...], axis=1, keepdims=True)
    own_row = jnp.sum(jnp.where(sub == lane, own_col, 0.0), axis=0, keepdims=True)
    message[...] = jnp.broadcast_to(own_row, message.shape)
    partials[shard] = message[...]

    def sum_copy(step):
        return pltpu.make_async_remote_copy(
            src_ref=message, dst_ref=partials.at[shard],
            send_sem=sum_send.at[step], recv_sem=sum_recv.at[step],
            device_id=(section, (shard + step) % shards), device_id_type=MESH,
        )

    for step in range(1, shards):
        sum_copy(step).start()

    def finish_sends(q):
        for step in range(1, depth_z):
            z_copy(q, step).wait_send()
        for kind in range(7):
            line_copy(q, kind).wait_send()

    finish_sends(None)
    pl.loop(0, chunks)(finish_sends)

    for step in range(1, shards):
        sum_copy(step).wait_recv()
    scores = partials[0]
    for other in range(1, shards):
        scores = scores + partials[other]
    scores = scores[:1, :]
    flipped = section % 2 == 1
    log_sigmoid = jnp.minimum(scores, 0.0) - jnp.log1p(jnp.exp(-jnp.abs(scores)))
    values = jnp.where(flipped, log_sigmoid, scores)
    value_col = jnp.sum(jnp.where(sub == lane, values, 0.0), axis=1, keepdims=True)

    lanes = lax.broadcasted_iota(jnp.int32, (total_rows, LANES), 1)
    own_count = joined_ref.shape[1]
    pack_rows = scores_ref.shape[1]

    def owned_by(sec):
        base = (sec * shards + shard) * own_count
        return jnp.sum(jnp.where(owner_col[...] == base + lanes, value_col, 0.0), axis=0, keepdims=True)

    def join_copy(step):
        return pltpu.make_async_remote_copy(
            src_ref=join_out.at[step], dst_ref=join_in.at[section],
            send_sem=join_send.at[step], recv_sem=join_recv.at[step],
            device_id=((section + step) % sections, shard), device_id_type=MESH,
        )

    for step in range(1, sections):
        join_out[step] = jnp.broadcast_to(owned_by((section + step) % sections), join_out.shape[1:])
        join_copy(step).start()
    join_in[section] = jnp.broadcast_to(owned_by(section), join_in.shape[1:])

    base = shard * pack_rows
    packed = jnp.sum(jnp.where(pack_col[...] == base + lanes, value_col, 0.0), axis=0, keepdims=True)
    scores_ref[...] = packed[:, :pack_rows]

    for step in range(1, sections):
        join_copy(step).wait_recv()
    for sec in range(sections):
        joined_ref[sec : sec + 1, :] = join_in[sec][:1, :own_count]

    for step in range(1, shards):
        sum_copy(step).wait_send()
    for step in range(1, sections):
        join_copy(step).wait_send()


def body(sections, shards, hidden, norm_gain, gate_weight, up_weight, head_vector, pack_slot, owner_slot):
    total_rows = owner_slot.shape[0]
    width = hidden.shape[1]
    own_units = head_vector.shape[1]
    half = width // CHUNKS // 2
    depth_z = shards // 2
    line_kinds = 7
    fixed = total_rows * (width * 2 + own_units * 8 + 2 * half * 2 + LANES * 4 * 4)
    fixed += shards * total_rows * 32 + 4 * 2**20
    slot_bytes = 2 * (width // CHUNKS) * own_units * 2
    slots = max(1, min(CHUNKS, (VMEM_BUDGET - fixed) // slot_bytes))
    vmem, dma = pltpu.VMEM, pltpu.SemaphoreType.DMA
    flops = 4 * total_rows * width * own_units
    return pl.pallas_call(
        functools.partial(kernel, sections, shards, slots),
        out_shape=(
            jax.ShapeDtypeStruct((1, total_rows // shards), jnp.float32),
            jax.ShapeDtypeStruct((sections, total_rows // (shards * sections)), jnp.float32),
        ),
        in_specs=[pl.BlockSpec(memory_space=vmem)] * 5 + [pl.BlockSpec(memory_space=pl.ANY)] * 2,
        out_specs=(pl.BlockSpec(memory_space=vmem), pl.BlockSpec(memory_space=vmem)),
        scratch_shapes=[
            vmem((CHUNKS, sections, depth_z, 2, 16, half), jnp.bfloat16),
            vmem((sections, depth_z, 2, 8, LANES), jnp.float32),
            vmem((slots, 2 * half, own_units), jnp.bfloat16),
            vmem((slots, 2 * half, own_units), jnp.bfloat16),
            vmem((total_rows, 2 * half), jnp.bfloat16),
            vmem((total_rows, own_units), jnp.float32),
            vmem((total_rows, own_units), jnp.float32),
            vmem((total_rows, LANES), jnp.float32),
            vmem((total_rows, 1), jnp.int32),
            vmem((total_rows, 1), jnp.int32),
            vmem((8, total_rows), jnp.float32),
            vmem((shards, 8, total_rows), jnp.float32),
            vmem((sections, 8, LANES), jnp.float32),
            vmem((sections, 8, LANES), jnp.float32),
            dma((slots, 2)),
            dma((CHUNKS + 1, line_kinds)),
            dma((CHUNKS + 1, line_kinds)),
            dma((CHUNKS + 1, depth_z)),
            dma((CHUNKS + 1, depth_z)),
            dma((shards,)),
            dma((shards,)),
            dma((sections,)),
            dma((sections,)),
        ],
        compiler_params=pltpu.CompilerParams(
            collective_id=0, has_side_effects=True, vmem_limit_bytes=VMEM_BUDGET + 3 * 2**20
        ),
        cost_estimate=pl.CostEstimate(
            flops=flops, bytes_accessed=4 * width * own_units, transcendentals=total_rows * own_units
        ),
    )(hidden, norm_gain, head_vector, pack_slot, owner_slot[None, :], gate_weight, up_weight)


def solution(mesh):
    in_specs = (
        P(("section", "shard"), None),
        P("section", None),
        P("section", None, "shard"),
        P("section", None, "shard"),
        P("section", "shard"),
        P(),
        P(),
    )
    out_specs = (P("section", "shard"), P(None, ("section", "shard")))
    run = functools.partial(body, mesh.shape["section"], mesh.shape["shard"])
    return jax.shard_map(run, mesh=mesh, in_specs=in_specs, out_specs=out_specs, check_vma=False)
```

```python
import functools

import jax
import jax.numpy as jnp
from jax import lax
from jax.experimental import pallas as pl
from jax.experimental.pallas import tpu as pltpu
from jax.sharding import PartitionSpec as P

epsilon = 1e-06
MESH = pl.DeviceIdType.MESH
CHUNKS = 8
COLUMN_TILE = 1024
UNIT_TILE = 256
EARLY_SLOTS = 2
ROW_TILE = 256
LANES = 128
VMEM_BUDGET = 58 * 2**20


def kernel(
    sections, shards, slots,
    hidden_ref, gain_ref, head_ref, pack_ref, owner_ref, gate_ref, up_ref,
    result_ref,
    rows_buf, inv_buf, gate_ring, up_ring, normed, gate_acc, up_acc, part,
    pack_col, owner_col, message, partials, join_out, join_in,
    ring_sem, line_send, line_recv, z_send, z_recv, sum_send, sum_recv, join_send, join_recv,
):
    chunks, _, depth_z, _, _, half = rows_buf.shape
    width = 2 * half
    total_rows = pack_ref.shape[1]
    own_units = head_ref.shape[1]
    section_rows = total_rows // sections

    section = lax.axis_index("section")
    shard = lax.axis_index("shard")
    x, core = section // 2, section % 2
    z, y = shard // 2, shard % 2
    across_x = (section + 2) % sections
    across_core = 2 * x + 1 - core
    across_y = 1 - y
    shard_y = 2 * z + across_y

    def weight_copies(q):
        slot = q % slots
        rows = pl.ds(pl.multiple_of(q * width, width), width)
        return (
            pltpu.make_async_copy(gate_ref.at[0, rows, :], gate_ring.at[slot], ring_sem.at[slot, 0]),
            pltpu.make_async_copy(up_ref.at[0, rows, :], up_ring.at[slot], ring_sem.at[slot, 1]),
        )

    def load_weights(q):
        for copy in weight_copies(q):
            copy.start()

    pl.loop(0, min(EARLY_SLOTS, slots))(load_weights)

    barrier = pltpu.get_barrier_semaphore()
    for step in range(1, shards):
        pl.semaphore_signal(barrier, inc=1, device_id=(section, (shard + step) % shards), device_id_type=MESH)
    for step in range(1, sections):
        pl.semaphore_signal(barrier, inc=1, device_id=((section + step) % sections, shard), device_id_type=MESH)

    widened = hidden_ref[...].astype(jnp.float32)
    inv = lax.rsqrt(jnp.mean(widened * widened, axis=1, keepdims=True) + epsilon)
    inv_buf[section, z, y] = jnp.broadcast_to(inv, inv_buf.shape[3:])
    for q in range(chunks):
        low = widened[:, q * width : q * width + half]
        high = widened[:, q * width + half : (q + 1) * width]
        rows_buf[q, section, z, y] = jnp.concatenate([low, high], axis=0).astype(jnp.bfloat16)

    pl.semaphore_wait(barrier, shards - 1 + sections - 1)

    def line(q, sec, row):
        return inv_buf.at[sec, :, row] if q is None else rows_buf.at[q, sec, :, row]

    def sem_row(q):
        return chunks if q is None else q

    def z_copy(q, step):
        block = inv_buf.at[section, z, y] if q is None else rows_buf.at[q, section, z, y]
        at = sem_row(q)
        return pltpu.make_async_remote_copy(
            src_ref=block, dst_ref=block,
            send_sem=z_send.at[at, step], recv_sem=z_recv.at[at, step],
            device_id=(section, 2 * ((z + step) % depth_z) + y), device_id_type=MESH,
        )

    def line_copy(q, kind):
        if kind == 0:
            source, target = (section, y), (across_x, shard)
        elif kind == 1:
            source, target = (section, y), (section, shard_y)
        elif kind == 2:
            odd = 0 if q is None else q % 2
            source = (across_x + odd * (section - across_x), y + odd * (across_y - y))
            target = (section + odd * (across_x - section), shard_y + odd * (shard - shard_y))
        else:
            source = ((section, y), (across_x, y), (section, across_y), (across_x, across_y))[kind - 3]
            target = (across_core, shard)
        part_line = line(q, *source)
        at = sem_row(q)
        return pltpu.make_async_remote_copy(
            src_ref=part_line, dst_ref=part_line,
            send_sem=line_send.at[at, kind], recv_sem=line_recv.at[at, kind],
            device_id=target, device_id_type=MESH,
        )

    def send_z(q):
        for step in range(1, depth_z):
            z_copy(q, step).start()

    def send_line(q):
        for step in range(1, depth_z):
            z_copy(q, step).wait_recv()
        for kind in (0, 1, 3):
            line_copy(q, kind).start()

    def forward_line(q):
        line_copy(q, 0).wait_recv()
        line_copy(q, 1).wait_recv()
        for kind in (2, 4, 5):
            line_copy(q, kind).start()

    def forward_diagonal(q):
        line_copy(q, 2).wait_recv()
        line_copy(q, 6).start()

    def collect(q):
        for kind in (3, 4, 5, 6):
            line_copy(q, kind).wait_recv()

    send_z(None)
    pl.loop(0, chunks)(send_z)
    pl.loop(min(EARLY_SLOTS, slots), slots)(load_weights)

    sub = lax.broadcasted_iota(jnp.int32, (total_rows, total_rows), 0)
    lane = lax.broadcasted_iota(jnp.int32, (total_rows, total_rows), 1)
    pack_row = pack_ref[pl.ds(section, 1), :]
    pack_col[...] = jnp.sum(jnp.where(sub == lane, pack_row, 0), axis=1, keepdims=True)
    owner_col[...] = jnp.sum(jnp.where(sub == lane, owner_ref[...], 0), axis=1, keepdims=True)

    row_tiles = total_rows // ROW_TILE
    column_tiles = own_units // COLUMN_TILE

    def tile(index):
        rows = pl.ds(pl.multiple_of((index // column_tiles) * ROW_TILE, ROW_TILE), ROW_TILE)
        columns = pl.ds(pl.multiple_of((index % column_tiles) * COLUMN_TILE, COLUMN_TILE), COLUMN_TILE)
        return rows, columns

    @pl.loop(0, row_tiles * column_tiles)
    def _(index):
        at = tile(index)
        gate_acc[at] = jnp.zeros((ROW_TILE, COLUMN_TILE), jnp.float32)
        up_acc[at] = jnp.zeros((ROW_TILE, COLUMN_TILE), jnp.float32)

    part[...] = jnp.zeros_like(part)

    def compute(q):
        for sec in range(sections):
            rows = slice(sec * section_rows, (sec + 1) * section_rows)
            inv_rows = inv_buf[sec].reshape(section_rows, LANES)
            for start in range(0, half, LANES):
                stacked = rows_buf[q, sec, :, :, :, start : start + LANES].astype(jnp.float32)
                for side in range(2):
                    at = side * half + start
                    columns = pl.ds(pl.multiple_of(q * width + at, LANES), LANES)
                    values = stacked[:, :, side * 8 : side * 8 + 8, :].reshape(section_rows, LANES)
                    scaled = values * inv_rows * gain_ref[:, columns]
                    normed[rows, at : at + LANES] = scaled.astype(jnp.bfloat16)
        for copy in weight_copies(q):
            copy.wait()
        slot = q % slots

        @pl.loop(0, row_tiles * column_tiles)
        def _(index):
            rows, _ = tile(index)
            left = normed[rows, :]
            first = (index % column_tiles) * COLUMN_TILE
            for start in range(0, COLUMN_TILE, UNIT_TILE):
                columns = pl.ds(pl.multiple_of(first + start, UNIT_TILE), UNIT_TILE)
                for ring, total in ((gate_ring, gate_acc), (up_ring, up_acc)):
                    total[rows, columns] += jnp.dot(
                        left, ring[slot, :, columns], preferred_element_type=jnp.float32
                    )

        @pl.when(q + slots < chunks)
        def _():
            load_weights(q + slots)

    @pl.loop(0, chunks + 3)
    def _(t):
        @pl.when(t == 0)
        def _():
            send_line(None)

        @pl.when(t < chunks)
        def _():
            send_line(t)

        @pl.when(t == 1)
        def _():
            forward_line(None)

        @pl.when(jnp.logical_and(t >= 1, t < chunks + 1))
        def _():
            forward_line(t - 1)

        @pl.when(t == 2)
        def _():
            forward_diagonal(None)

        @pl.when(jnp.logical_and(t >= 2, t < chunks + 2))
        def _():
            forward_diagonal(t - 2)

        @pl.when(t == 3)
        def _():
            collect(None)

        @pl.when(t >= 3)
        def _():
            collect(t - 3)
            compute(t - 3)

    @pl.loop(0, row_tiles * (own_units // LANES))
    def _(index):
        per_row = own_units // LANES
        rows = pl.ds(pl.multiple_of((index // per_row) * ROW_TILE, ROW_TILE), ROW_TILE)
        columns = pl.ds(pl.multiple_of((index % per_row) * LANES, LANES), LANES)
        gate = gate_acc[rows, columns]
        activated = gate / (1.0 + jnp.exp(-gate)) * up_acc[rows, columns]
        part[rows, :] += activated * head_ref[:, columns].astype(jnp.float32)

    own_col = jnp.sum(part[...], axis=1, keepdims=True)
    own_row = jnp.sum(jnp.where(sub == lane, own_col, 0.0), axis=0, keepdims=True)
    message[...] = jnp.broadcast_to(own_row, message.shape)
    partials[shard] = message[...]

    def sum_copy(step):
        return pltpu.make_async_remote_copy(
            src_ref=message, dst_ref=partials.at[shard],
            send_sem=sum_send.at[step], recv_sem=sum_recv.at[step],
            device_id=(section, (shard + step) % shards), device_id_type=MESH,
        )

    for step in range(1, shards):
        sum_copy(step).start()

    def finish_sends(q):
        for step in range(1, depth_z):
            z_copy(q, step).wait_send()
        for kind in range(7):
            line_copy(q, kind).wait_send()

    finish_sends(None)
    pl.loop(0, chunks)(finish_sends)

    for step in range(1, shards):
        sum_copy(step).wait_recv()
    scores = partials[0]
    for other in range(1, shards):
        scores = scores + partials[other]
    scores = scores[:1, :]
    flipped = section % 2 == 1
    log_sigmoid = jnp.minimum(scores, 0.0) - jnp.log1p(jnp.exp(-jnp.abs(scores)))
    values = jnp.where(flipped, log_sigmoid, scores)
    value_col = jnp.sum(jnp.where(sub == lane, values, 0.0), axis=1, keepdims=True)

    lanes = lax.broadcasted_iota(jnp.int32, (total_rows, LANES), 1)
    own_count = total_rows // (sections * shards)
    pack_rows = total_rows // shards

    def owned_by(sec):
        base = (sec * shards + shard) * own_count
        return jnp.sum(jnp.where(owner_col[...] == base + lanes, value_col, 0.0), axis=0, keepdims=True)

    def join_copy(step):
        return pltpu.make_async_remote_copy(
            src_ref=join_out.at[step], dst_ref=join_in.at[section],
            send_sem=join_send.at[step], recv_sem=join_recv.at[step],
            device_id=((section + step) % sections, shard), device_id_type=MESH,
        )

    for step in range(1, sections):
        join_out[step] = jnp.broadcast_to(owned_by((section + step) % sections), join_out.shape[1:])
        join_copy(step).start()
    join_in[section] = jnp.broadcast_to(owned_by(section), join_in.shape[1:])

    base = shard * pack_rows
    packed = jnp.sum(jnp.where(pack_col[...] == base + lanes, value_col, 0.0), axis=0, keepdims=True)
    result_ref[sections:, :] = jnp.broadcast_to(packed, (result_ref.shape[0] - sections, LANES))

    for step in range(1, sections):
        join_copy(step).wait_recv()
    for sec in range(sections):
        result_ref[sec : sec + 1, :] = join_in[sec][:1, :]

    for step in range(1, shards):
        sum_copy(step).wait_send()
    for step in range(1, sections):
        join_copy(step).wait_send()


def body(sections, shards, hidden, norm_gain, gate_weight, up_weight, head_vector, pack_slot, owner_slot):
    total_rows = owner_slot.shape[0]
    width = hidden.shape[1]
    own_units = head_vector.shape[1]
    half = width // CHUNKS // 2
    depth_z = shards // 2
    line_kinds = 7
    fixed = total_rows * (width * 2 + own_units * 8 + 2 * half * 2 + LANES * 4 * 4)
    fixed += shards * total_rows * 32 + 4 * 2**20
    slot_bytes = 2 * (width // CHUNKS) * own_units * 2
    slots = max(1, min(CHUNKS, (VMEM_BUDGET - fixed) // slot_bytes))
    vmem, dma = pltpu.VMEM, pltpu.SemaphoreType.DMA
    flops = 4 * total_rows * width * own_units
    result = pl.pallas_call(
        functools.partial(kernel, sections, shards, slots),
        out_shape=jax.ShapeDtypeStruct((2 * sections, LANES), jnp.float32),
        in_specs=[pl.BlockSpec(memory_space=vmem)] * 5 + [pl.BlockSpec(memory_space=pl.ANY)] * 2,
        out_specs=pl.BlockSpec(memory_space=vmem),
        scratch_shapes=[
            vmem((CHUNKS, sections, depth_z, 2, 16, half), jnp.bfloat16),
            vmem((sections, depth_z, 2, 8, LANES), jnp.float32),
            vmem((slots, 2 * half, own_units), jnp.bfloat16),
            vmem((slots, 2 * half, own_units), jnp.bfloat16),
            vmem((total_rows, 2 * half), jnp.bfloat16),
            vmem((total_rows, own_units), jnp.float32),
            vmem((total_rows, own_units), jnp.float32),
            vmem((total_rows, LANES), jnp.float32),
            vmem((total_rows, 1), jnp.int32),
            vmem((total_rows, 1), jnp.int32),
            vmem((8, total_rows), jnp.float32),
            vmem((shards, 8, total_rows), jnp.float32),
            vmem((sections, 8, LANES), jnp.float32),
            vmem((sections, 8, LANES), jnp.float32),
            dma((slots, 2)),
            dma((CHUNKS + 1, line_kinds)),
            dma((CHUNKS + 1, line_kinds)),
            dma((CHUNKS + 1, depth_z)),
            dma((CHUNKS + 1, depth_z)),
            dma((shards,)),
            dma((shards,)),
            dma((sections,)),
            dma((sections,)),
        ],
        compiler_params=pltpu.CompilerParams(
            collective_id=0, has_side_effects=True, vmem_limit_bytes=VMEM_BUDGET + 3 * 2**20
        ),
        cost_estimate=pl.CostEstimate(
            flops=flops, bytes_accessed=4 * width * own_units, transcendentals=total_rows * own_units
        ),
    )(hidden, norm_gain, head_vector, pack_slot, owner_slot[None, :], gate_weight, up_weight)
    return (
        result[sections : sections + 1, : total_rows // shards],
        result[:sections, : total_rows // (sections * shards)],
    )


def solution(mesh):
    in_specs = (
        P(("section", "shard"), None),
        P("section", None),
        P("section", None, "shard"),
        P("section", None, "shard"),
        P("section", "shard"),
        P(),
        P(),
    )
    out_specs = (P("section", "shard"), P(None, ("section", "shard")))
    run = functools.partial(body, mesh.shape["section"], mesh.shape["shard"])
    return jax.shard_map(run, mesh=mesh, in_specs=in_specs, out_specs=out_specs, check_vma=False)
```

```python
import functools

import jax
import jax.numpy as jnp
from jax import lax
from jax.experimental import pallas as pl
from jax.experimental.pallas import tpu as pltpu
from jax.sharding import PartitionSpec as P

epsilon = 1e-06
MESH = pl.DeviceIdType.MESH
CHUNKS = 16
GROUP = 2
UNIT_TILE = 256
EARLY_SLOTS = 2
ROW_TILE = 256
LANES = 128
VMEM_BUDGET = 58 * 2**20


def kernel(
    sections, shards, slots,
    hidden_ref, gain_ref, head_ref, pack_ref, owner_ref, gate_ref, up_ref,
    result_ref,
    rows_buf, inv_buf, gate_ring, up_ring, normed, gate_acc, up_acc, part,
    pack_col, owner_col, message, partials, join_out, join_in,
    ring_sem, line_send, line_recv, z_send, z_recv, sum_send, sum_recv, join_send, join_recv,
):
    chunks, _, depth_z, _, _, half = rows_buf.shape
    width = 2 * half
    depth = GROUP * width
    total_rows = pack_ref.shape[1]
    own_units = head_ref.shape[1]
    section_rows = total_rows // sections

    section = lax.axis_index("section")
    shard = lax.axis_index("shard")
    x, core = section // 2, section % 2
    z, y = shard // 2, shard % 2
    across_x = (section + 2) % sections
    across_core = 2 * x + 1 - core
    across_y = 1 - y
    shard_y = 2 * z + across_y

    def weight_copies(q):
        slot = q % slots
        rows = pl.ds(pl.multiple_of(q * depth, depth), depth)
        return (
            pltpu.make_async_copy(gate_ref.at[0, rows, :], gate_ring.at[slot], ring_sem.at[slot, 0]),
            pltpu.make_async_copy(up_ref.at[0, rows, :], up_ring.at[slot], ring_sem.at[slot, 1]),
        )

    def load_weights(q):
        for copy in weight_copies(q):
            copy.start()

    pl.loop(0, min(EARLY_SLOTS, slots))(load_weights)

    barrier = pltpu.get_barrier_semaphore()
    for step in range(1, shards):
        pl.semaphore_signal(barrier, inc=1, device_id=(section, (shard + step) % shards), device_id_type=MESH)
    for step in range(1, sections):
        pl.semaphore_signal(barrier, inc=1, device_id=((section + step) % sections, shard), device_id_type=MESH)

    widened = hidden_ref[...].astype(jnp.float32)
    inv = lax.rsqrt(jnp.mean(widened * widened, axis=1, keepdims=True) + epsilon)
    inv_buf[section, z, y] = jnp.broadcast_to(inv, inv_buf.shape[3:])
    for q in range(chunks):
        low = widened[:, q * width : q * width + half]
        high = widened[:, q * width + half : (q + 1) * width]
        rows_buf[q, section, z, y] = jnp.concatenate([low, high], axis=0).astype(jnp.bfloat16)

    pl.semaphore_wait(barrier, shards - 1 + sections - 1)

    def line(q, sec, row):
        return inv_buf.at[sec, :, row] if q is None else rows_buf.at[q, sec, :, row]

    def sem_row(q):
        return chunks if q is None else q

    def z_copy(q, step):
        block = inv_buf.at[section, z, y] if q is None else rows_buf.at[q, section, z, y]
        at = sem_row(q)
        return pltpu.make_async_remote_copy(
            src_ref=block, dst_ref=block,
            send_sem=z_send.at[at, step], recv_sem=z_recv.at[at, step],
            device_id=(section, 2 * ((z + step) % depth_z) + y), device_id_type=MESH,
        )

    def line_copy(q, kind):
        if kind == 0:
            source, target = (section, y), (across_x, shard)
        elif kind == 1:
            source, target = (section, y), (section, shard_y)
        elif kind == 2:
            odd = 0 if q is None else q % 2
            source = (across_x + odd * (section - across_x), y + odd * (across_y - y))
            target = (section + odd * (across_x - section), shard_y + odd * (shard - shard_y))
        else:
            source = ((section, y), (across_x, y), (section, across_y), (across_x, across_y))[kind - 3]
            target = (across_core, shard)
        part_line = line(q, *source)
        at = sem_row(q)
        return pltpu.make_async_remote_copy(
            src_ref=part_line, dst_ref=part_line,
            send_sem=line_send.at[at, kind], recv_sem=line_recv.at[at, kind],
            device_id=target, device_id_type=MESH,
        )

    def send_z(q):
        for step in range(1, depth_z):
            z_copy(q, step).start()

    def send_line(q):
        for step in range(1, depth_z):
            z_copy(q, step).wait_recv()
        for kind in (0, 1, 3):
            line_copy(q, kind).start()

    def forward_line(q):
        line_copy(q, 0).wait_recv()
        line_copy(q, 1).wait_recv()
        for kind in (2, 4, 5):
            line_copy(q, kind).start()

    def forward_diagonal(q):
        line_copy(q, 2).wait_recv()
        line_copy(q, 6).start()

    def collect(q):
        for kind in (3, 4, 5, 6):
            line_copy(q, kind).wait_recv()

    send_z(None)
    pl.loop(0, chunks)(send_z)
    pl.loop(min(EARLY_SLOTS, slots), slots)(load_weights)

    sub = lax.broadcasted_iota(jnp.int32, (total_rows, total_rows), 0)
    lane = lax.broadcasted_iota(jnp.int32, (total_rows, total_rows), 1)
    pack_row = pack_ref[pl.ds(section, 1), :]
    pack_col[...] = jnp.sum(jnp.where(sub == lane, pack_row, 0), axis=1, keepdims=True)
    owner_col[...] = jnp.sum(jnp.where(sub == lane, owner_ref[...], 0), axis=1, keepdims=True)

    row_tiles = total_rows // ROW_TILE

    @pl.loop(0, total_rows // ROW_TILE)
    def _(index):
        rows = pl.ds(pl.multiple_of(index * ROW_TILE, ROW_TILE), ROW_TILE)
        gate_acc[rows, :] = jnp.zeros((ROW_TILE, own_units), jnp.float32)
        up_acc[rows, :] = jnp.zeros((ROW_TILE, own_units), jnp.float32)

    part[...] = jnp.zeros_like(part)

    steps = chunks // GROUP
    half_units = own_units // 2

    def normalise(q, place):
        for sec in range(sections):
            rows = slice(sec * section_rows, (sec + 1) * section_rows)
            inv_rows = inv_buf[sec].reshape(section_rows, LANES)
            for start in range(0, half, LANES):
                stacked = rows_buf[q, sec, :, :, :, start : start + LANES].astype(jnp.float32)
                for side in range(2):
                    at = side * half + start
                    columns = pl.ds(pl.multiple_of(q * width + at, LANES), LANES)
                    values = stacked[:, :, side * 8 : side * 8 + 8, :].reshape(section_rows, LANES)
                    scaled = values * inv_rows * gain_ref[:, columns]
                    normed[rows, place * width + at : place * width + at + LANES] = scaled.astype(jnp.bfloat16)

    def prepare(step):
        for place in range(GROUP):
            normalise(step * GROUP + place, place)
        for copy in weight_copies(step):
            copy.wait()

    def multiply(step, side):
        slot = step % slots

        def row_tile(index):
            rows = pl.ds(pl.multiple_of(index * ROW_TILE, ROW_TILE), ROW_TILE)
            left = normed[rows, :]
            for start in range(0, half_units, UNIT_TILE):
                columns = pl.ds(pl.multiple_of(side * half_units + start, UNIT_TILE), UNIT_TILE)
                for ring, total in ((gate_ring, gate_acc), (up_ring, up_acc)):
                    total[rows, columns] += jnp.dot(
                        left, ring[slot, :, columns], preferred_element_type=jnp.float32
                    )

        pl.loop(0, row_tiles)(row_tile)

    send_line(None)
    send_line(0)
    forward_line(None)
    send_line(1)
    forward_line(0)
    forward_diagonal(None)
    send_line(2)
    forward_line(1)
    forward_diagonal(0)
    send_line(3)
    forward_line(2)
    forward_diagonal(1)
    collect(None)
    collect(0)
    send_line(4)
    forward_line(3)
    forward_diagonal(2)
    collect(1)

    @pl.loop(0, 2 * steps)
    def _(u):
        def advance(act, q, limit):
            @pl.when(jnp.logical_and(u > 0, jnp.logical_and(q < limit, q < chunks)))
            def _():
                act(q)

        for ahead in range(2):
            advance(send_line, 3 + 2 * u + ahead, 5 + 2 * u)
        for ahead in range(2):
            advance(forward_line, 4 + (3 * (u - 1 + steps * 2)) // 2 - 3 * steps + ahead, 4 + (3 * u) // 2)
        for ahead in range(2):
            advance(forward_diagonal, 3 + (5 * (u + 3)) // 4 - 5 + ahead, 3 + (5 * u) // 4)
        advance(collect, u + 1, u + 2)

        step, side = u // 2, u % 2

        @pl.when(side == 0)
        def _():
            prepare(step)

        multiply(step, side)

        @pl.when(jnp.logical_and(side == 1, step + slots < steps))
        def _():
            load_weights(step + slots)

    @pl.loop(0, row_tiles * (own_units // LANES))
    def _(index):
        per_row = own_units // LANES
        rows = pl.ds(pl.multiple_of((index // per_row) * ROW_TILE, ROW_TILE), ROW_TILE)
        columns = pl.ds(pl.multiple_of((index % per_row) * LANES, LANES), LANES)
        gate = gate_acc[rows, columns]
        activated = gate / (1.0 + jnp.exp(-gate)) * up_acc[rows, columns]
        part[rows, :] += activated * head_ref[:, columns].astype(jnp.float32)

    own_col = jnp.sum(part[...], axis=1, keepdims=True)
    own_row = jnp.sum(jnp.where(sub == lane, own_col, 0.0), axis=0, keepdims=True)
    message[...] = jnp.broadcast_to(own_row, message.shape)
    partials[shard] = message[...]

    def sum_copy(step):
        return pltpu.make_async_remote_copy(
            src_ref=message, dst_ref=partials.at[shard],
            send_sem=sum_send.at[step], recv_sem=sum_recv.at[step],
            device_id=(section, (shard + step) % shards), device_id_type=MESH,
        )

    for step in range(1, shards):
        sum_copy(step).start()

    def finish_sends(q):
        for step in range(1, depth_z):
            z_copy(q, step).wait_send()
        for kind in range(7):
            line_copy(q, kind).wait_send()

    finish_sends(None)
    pl.loop(0, chunks)(finish_sends)

    for step in range(1, shards):
        sum_copy(step).wait_recv()
    scores = partials[0]
    for other in range(1, shards):
        scores = scores + partials[other]
    scores = scores[:1, :]
    flipped = section % 2 == 1
    log_sigmoid = jnp.minimum(scores, 0.0) - jnp.log1p(jnp.exp(-jnp.abs(scores)))
    values = jnp.where(flipped, log_sigmoid, scores)
    value_col = jnp.sum(jnp.where(sub == lane, values, 0.0), axis=1, keepdims=True)

    lanes = lax.broadcasted_iota(jnp.int32, (total_rows, LANES), 1)
    own_count = total_rows // (sections * shards)
    pack_rows = total_rows // shards

    def owned_by(sec):
        base = (sec * shards + shard) * own_count
        return jnp.sum(jnp.where(owner_col[...] == base + lanes, value_col, 0.0), axis=0, keepdims=True)

    def join_copy(step):
        return pltpu.make_async_remote_copy(
            src_ref=join_out.at[step], dst_ref=join_in.at[section],
            send_sem=join_send.at[step], recv_sem=join_recv.at[step],
            device_id=((section + step) % sections, shard), device_id_type=MESH,
        )

    for step in range(1, sections):
        join_out[step] = jnp.broadcast_to(owned_by((section + step) % sections), join_out.shape[1:])
        join_copy(step).start()
    join_in[section] = jnp.broadcast_to(owned_by(section), join_in.shape[1:])

    base = shard * pack_rows
    packed = jnp.sum(jnp.where(pack_col[...] == base + lanes, value_col, 0.0), axis=0, keepdims=True)
    result_ref[sections:, :] = jnp.broadcast_to(packed, (result_ref.shape[0] - sections, LANES))

    for step in range(1, sections):
        join_copy(step).wait_recv()
    for sec in range(sections):
        result_ref[sec : sec + 1, :] = join_in[sec][:1, :]

    for step in range(1, shards):
        sum_copy(step).wait_send()
    for step in range(1, sections):
        join_copy(step).wait_send()


def body(sections, shards, hidden, norm_gain, gate_weight, up_weight, head_vector, pack_slot, owner_slot):
    total_rows = owner_slot.shape[0]
    width = hidden.shape[1]
    own_units = head_vector.shape[1]
    half = width // CHUNKS // 2
    depth_z = shards // 2
    line_kinds = 7
    fixed = total_rows * (width * 2 + own_units * 8 + 2 * half * 2 + LANES * 4 * 4)
    fixed += shards * total_rows * 32 + 4 * 2**20
    slot_bytes = 2 * GROUP * (width // CHUNKS) * own_units * 2
    slots = max(1, min(CHUNKS // GROUP, (VMEM_BUDGET - fixed) // slot_bytes))
    vmem, dma = pltpu.VMEM, pltpu.SemaphoreType.DMA
    flops = 4 * total_rows * width * own_units
    result = pl.pallas_call(
        functools.partial(kernel, sections, shards, slots),
        out_shape=jax.ShapeDtypeStruct((2 * sections, LANES), jnp.float32),
        in_specs=[pl.BlockSpec(memory_space=vmem)] * 5 + [pl.BlockSpec(memory_space=pl.ANY)] * 2,
        out_specs=pl.BlockSpec(memory_space=vmem),
        scratch_shapes=[
            vmem((CHUNKS, sections, depth_z, 2, 16, half), jnp.bfloat16),
            vmem((sections, depth_z, 2, 8, LANES), jnp.float32),
            vmem((slots, GROUP * 2 * half, own_units), jnp.bfloat16),
            vmem((slots, GROUP * 2 * half, own_units), jnp.bfloat16),
            vmem((total_rows, GROUP * 2 * half), jnp.bfloat16),
            vmem((total_rows, own_units), jnp.float32),
            vmem((total_rows, own_units), jnp.float32),
            vmem((total_rows, LANES), jnp.float32),
            vmem((total_rows, 1), jnp.int32),
            vmem((total_rows, 1), jnp.int32),
            vmem((8, total_rows), jnp.float32),
            vmem((shards, 8, total_rows), jnp.float32),
            vmem((sections, 8, LANES), jnp.float32),
            vmem((sections, 8, LANES), jnp.float32),
            dma((slots, 2)),
            dma((CHUNKS + 1, line_kinds)),
            dma((CHUNKS + 1, line_kinds)),
            dma((CHUNKS + 1, depth_z)),
            dma((CHUNKS + 1, depth_z)),
            dma((shards,)),
            dma((shards,)),
            dma((sections,)),
            dma((sections,)),
        ],
        compiler_params=pltpu.CompilerParams(
            collective_id=0, has_side_effects=True, vmem_limit_bytes=VMEM_BUDGET + 3 * 2**20
        ),
        cost_estimate=pl.CostEstimate(
            flops=flops, bytes_accessed=4 * width * own_units, transcendentals=total_rows * own_units
        ),
    )(hidden, norm_gain, head_vector, pack_slot, owner_slot[None, :], gate_weight, up_weight)
    return (
        result[sections : sections + 1, : total_rows // shards],
        result[:sections, : total_rows // (sections * shards)],
    )


def solution(mesh):
    in_specs = (
        P(("section", "shard"), None),
        P("section", None),
        P("section", None, "shard"),
        P("section", None, "shard"),
        P("section", "shard"),
        P(),
        P(),
    )
    out_specs = (P("section", "shard"), P(None, ("section", "shard")))
    run = functools.partial(body, mesh.shape["section"], mesh.shape["shard"])
    return jax.shard_map(run, mesh=mesh, in_specs=in_specs, out_specs=out_specs, check_vma=False)
```

```python
import functools

import jax
import jax.numpy as jnp
from jax import lax
from jax.experimental import pallas as pl
from jax.experimental.pallas import tpu as pltpu
from jax.sharding import PartitionSpec as P

epsilon = 1e-06
MESH = pl.DeviceIdType.MESH
CHUNKS = 8
COLUMN_TILE = 1024
UNIT_TILE = 512
EARLY_SLOTS = 2
ROW_TILE = 256
LANES = 128
VMEM_BUDGET = 58 * 2**20


def kernel(
    sections, shards, slots,
    hidden_ref, gain_ref, head_ref, pack_ref, owner_ref, gate_ref, up_ref,
    result_ref,
    rows_buf, inv_buf, gate_ring, up_ring, normed, gate_acc, up_acc, part,
    pack_col, owner_col, message, partials, join_out, join_in,
    ring_sem, line_send, line_recv, z_send, z_recv, sum_send, sum_recv, join_send, join_recv,
):
    chunks, _, _, depth_z, _, half = rows_buf.shape
    width = 2 * half
    total_rows = pack_ref.shape[1]
    own_units = head_ref.shape[1]
    section_rows = total_rows // sections

    section = lax.axis_index("section")
    shard = lax.axis_index("shard")
    x, core = section // 2, section % 2
    z, y = shard // 2, shard % 2
    across_x = (section + 2) % sections
    across_core = 2 * x + 1 - core
    across_y = 1 - y
    shard_y = 2 * z + across_y

    def weight_copies(q):
        slot = q % slots
        rows = pl.ds(pl.multiple_of(q * width, width), width)
        return (
            pltpu.make_async_copy(gate_ref.at[0, rows, :], gate_ring.at[slot], ring_sem.at[slot, 0]),
            pltpu.make_async_copy(up_ref.at[0, rows, :], up_ring.at[slot], ring_sem.at[slot, 1]),
        )

    def load_weights(q):
        for copy in weight_copies(q):
            copy.start()

    pl.loop(0, min(EARLY_SLOTS, slots))(load_weights)

    barrier = pltpu.get_barrier_semaphore()
    for step in range(1, shards):
        pl.semaphore_signal(barrier, inc=1, device_id=(section, (shard + step) % shards), device_id_type=MESH)
    for step in range(1, sections):
        pl.semaphore_signal(barrier, inc=1, device_id=((section + step) % sections, shard), device_id_type=MESH)

    widened = hidden_ref[...].astype(jnp.float32)
    inv = lax.rsqrt(jnp.mean(widened * widened, axis=1, keepdims=True) + epsilon)
    inv_buf[section, y, z] = jnp.broadcast_to(inv, inv_buf.shape[3:])
    for q in range(chunks):
        low = widened[:, q * width : q * width + half]
        high = widened[:, q * width + half : (q + 1) * width]
        rows_buf[q, section, y, z] = jnp.concatenate([low, high], axis=0).astype(jnp.bfloat16)

    pl.semaphore_wait(barrier, shards - 1 + sections - 1)

    def line(q, sec, row):
        return inv_buf.at[sec, row] if q is None else rows_buf.at[q, sec, row]

    def plane(q, sec):
        return inv_buf.at[sec] if q is None else rows_buf.at[q, sec]

    def sem_row(q):
        return chunks if q is None else q

    def z_copy(q, step):
        block = inv_buf.at[section, y, z] if q is None else rows_buf.at[q, section, y, z]
        at = sem_row(q)
        return pltpu.make_async_remote_copy(
            src_ref=block, dst_ref=block,
            send_sem=z_send.at[at, step], recv_sem=z_recv.at[at, step],
            device_id=(section, 2 * ((z + step) % depth_z) + y), device_id_type=MESH,
        )

    def line_copy(q, kind):
        if kind == 0:
            source, target = line(q, section, y), (across_x, shard)
        elif kind == 1:
            source, target = line(q, section, y), (section, shard_y)
        elif kind == 2:
            odd = 0 if q is None else q % 2
            source = line(q, across_x + odd * (section - across_x), y + odd * (across_y - y))
            target = (section + odd * (across_x - section), shard_y + odd * (shard - shard_y))
        else:
            source = plane(q, section if kind == 3 else across_x)
            target = (across_core, shard)
        at = sem_row(q)
        return pltpu.make_async_remote_copy(
            src_ref=source, dst_ref=source,
            send_sem=line_send.at[at, kind], recv_sem=line_recv.at[at, kind],
            device_id=target, device_id_type=MESH,
        )

    def send_z(q):
        for step in range(1, depth_z):
            z_copy(q, step).start()

    def send_line(q):
        for step in range(1, depth_z):
            z_copy(q, step).wait_recv()
        for kind in (0, 1):
            line_copy(q, kind).start()

    def forward_line(q):
        line_copy(q, 0).wait_recv()
        line_copy(q, 1).wait_recv()
        for kind in (2, 3):
            line_copy(q, kind).start()

    def forward_diagonal(q):
        line_copy(q, 2).wait_recv()
        line_copy(q, 4).start()

    def collect(q):
        for kind in (3, 4):
            line_copy(q, kind).wait_recv()

    send_z(None)
    pl.loop(0, chunks)(send_z)
    pl.loop(min(EARLY_SLOTS, slots), slots)(load_weights)

    sub = lax.broadcasted_iota(jnp.int32, (total_rows, total_rows), 0)
    lane = lax.broadcasted_iota(jnp.int32, (total_rows, total_rows), 1)
    in_section = sub % section_rows
    held_z, held_y = in_section // 8 % depth_z, in_section // (8 * depth_z)
    token = sub - in_section + (2 * held_z + held_y) * 8 + sub % 8
    pack_row = pack_ref[pl.ds(section, 1), :]
    pack_col[...] = jnp.sum(jnp.where(token == lane, pack_row, 0), axis=1, keepdims=True)
    owner_col[...] = jnp.sum(jnp.where(token == lane, owner_ref[...], 0), axis=1, keepdims=True)

    row_tiles = total_rows // ROW_TILE
    column_tiles = own_units // COLUMN_TILE

    def tile(index):
        rows = pl.ds(pl.multiple_of((index // column_tiles) * ROW_TILE, ROW_TILE), ROW_TILE)
        columns = pl.ds(pl.multiple_of((index % column_tiles) * COLUMN_TILE, COLUMN_TILE), COLUMN_TILE)
        return rows, columns

    @pl.loop(0, row_tiles * column_tiles)
    def _(index):
        at = tile(index)
        gate_acc[at] = jnp.zeros((ROW_TILE, COLUMN_TILE), jnp.float32)
        up_acc[at] = jnp.zeros((ROW_TILE, COLUMN_TILE), jnp.float32)

    part[...] = jnp.zeros_like(part)

    def compute(q):
        for sec in range(sections):
            rows = slice(sec * section_rows, (sec + 1) * section_rows)
            inv_rows = inv_buf[sec].reshape(section_rows, LANES)
            for start in range(0, half, LANES):
                stacked = rows_buf[q, sec, :, :, :, start : start + LANES].astype(jnp.float32)
                for side in range(2):
                    at = side * half + start
                    columns = pl.ds(pl.multiple_of(q * width + at, LANES), LANES)
                    values = stacked[:, :, side * 8 : side * 8 + 8, :].reshape(section_rows, LANES)
                    scaled = values * inv_rows * gain_ref[:, columns]
                    normed[rows, at : at + LANES] = scaled.astype(jnp.bfloat16)
        for copy in weight_copies(q):
            copy.wait()
        slot = q % slots

        @pl.loop(0, row_tiles * column_tiles)
        def _(index):
            rows, _ = tile(index)
            left = normed[rows, :]
            first = (index % column_tiles) * COLUMN_TILE
            for start in range(0, COLUMN_TILE, UNIT_TILE):
                columns = pl.ds(pl.multiple_of(first + start, UNIT_TILE), UNIT_TILE)
                for ring, total in ((gate_ring, gate_acc), (up_ring, up_acc)):
                    total[rows, columns] += jnp.dot(
                        left, ring[slot, :, columns], preferred_element_type=jnp.float32
                    )

        @pl.when(q + slots < chunks)
        def _():
            load_weights(q + slots)

    @pl.loop(0, chunks + 3)
    def _(t):
        @pl.when(t == 0)
        def _():
            send_line(None)

        @pl.when(t < chunks)
        def _():
            send_line(t)

        @pl.when(t == 1)
        def _():
            forward_line(None)

        @pl.when(jnp.logical_and(t >= 1, t < chunks + 1))
        def _():
            forward_line(t - 1)

        @pl.when(t == 2)
        def _():
            forward_diagonal(None)

        @pl.when(jnp.logical_and(t >= 2, t < chunks + 2))
        def _():
            forward_diagonal(t - 2)

        @pl.when(t == 3)
        def _():
            collect(None)

        @pl.when(t >= 3)
        def _():
            collect(t - 3)
            compute(t - 3)

    @pl.loop(0, row_tiles * (own_units // LANES))
    def _(index):
        per_row = own_units // LANES
        rows = pl.ds(pl.multiple_of((index // per_row) * ROW_TILE, ROW_TILE), ROW_TILE)
        columns = pl.ds(pl.multiple_of((index % per_row) * LANES, LANES), LANES)
        gate = gate_acc[rows, columns]
        activated = gate / (1.0 + jnp.exp(-gate)) * up_acc[rows, columns]
        part[rows, :] += activated * head_ref[:, columns].astype(jnp.float32)

    own_col = jnp.sum(part[...], axis=1, keepdims=True)
    own_row = jnp.sum(jnp.where(sub == lane, own_col, 0.0), axis=0, keepdims=True)
    message[...] = jnp.broadcast_to(own_row, message.shape)
    partials[shard] = message[...]

    def sum_copy(step):
        return pltpu.make_async_remote_copy(
            src_ref=message, dst_ref=partials.at[shard],
            send_sem=sum_send.at[step], recv_sem=sum_recv.at[step],
            device_id=(section, (shard + step) % shards), device_id_type=MESH,
        )

    for step in range(1, shards):
        sum_copy(step).start()

    def finish_sends(q):
        for step in range(1, depth_z):
            z_copy(q, step).wait_send()
        for kind in range(5):
            line_copy(q, kind).wait_send()

    finish_sends(None)
    pl.loop(0, chunks)(finish_sends)

    for step in range(1, shards):
        sum_copy(step).wait_recv()
    scores = partials[0]
    for other in range(1, shards):
        scores = scores + partials[other]
    scores = scores[:1, :]
    flipped = section % 2 == 1
    log_sigmoid = jnp.minimum(scores, 0.0) - jnp.log1p(jnp.exp(-jnp.abs(scores)))
    values = jnp.where(flipped, log_sigmoid, scores)
    value_col = jnp.sum(jnp.where(sub == lane, values, 0.0), axis=1, keepdims=True)

    lanes = lax.broadcasted_iota(jnp.int32, (total_rows, LANES), 1)
    own_count = total_rows // (sections * shards)
    pack_rows = total_rows // shards

    def owned_by(sec):
        base = (sec * shards + shard) * own_count
        return jnp.sum(jnp.where(owner_col[...] == base + lanes, value_col, 0.0), axis=0, keepdims=True)

    def join_copy(step):
        return pltpu.make_async_remote_copy(
            src_ref=join_out.at[step], dst_ref=join_in.at[section],
            send_sem=join_send.at[step], recv_sem=join_recv.at[step],
            device_id=((section + step) % sections, shard), device_id_type=MESH,
        )

    for step in range(1, sections):
        join_out[step] = jnp.broadcast_to(owned_by((section + step) % sections), join_out.shape[1:])
        join_copy(step).start()
    join_in[section] = jnp.broadcast_to(owned_by(section), join_in.shape[1:])

    base = shard * pack_rows
    packed = jnp.sum(jnp.where(pack_col[...] == base + lanes, value_col, 0.0), axis=0, keepdims=True)
    result_ref[sections:, :] = jnp.broadcast_to(packed, (result_ref.shape[0] - sections, LANES))

    for step in range(1, sections):
        join_copy(step).wait_recv()
    for sec in range(sections):
        result_ref[sec : sec + 1, :] = join_in[sec][:1, :]

    for step in range(1, shards):
        sum_copy(step).wait_send()
    for step in range(1, sections):
        join_copy(step).wait_send()


def part_result(result_ref, scores_ref, joined_ref):
    sections = joined_ref.shape[0]
    scores_ref[...] = result_ref[sections : sections + 1, : scores_ref.shape[1]]
    joined_ref[...] = result_ref[:sections, : joined_ref.shape[1]]


def body(sections, shards, hidden, norm_gain, gate_weight, up_weight, head_vector, pack_slot, owner_slot):
    total_rows = owner_slot.shape[0]
    width = hidden.shape[1]
    own_units = head_vector.shape[1]
    half = width // CHUNKS // 2
    depth_z = shards // 2
    line_kinds = 5
    fixed = total_rows * (width * 2 + own_units * 8 + 2 * half * 2 + LANES * 4 * 4)
    fixed += shards * total_rows * 32 + 4 * 2**20
    slot_bytes = 2 * (width // CHUNKS) * own_units * 2
    slots = max(1, min(CHUNKS, (VMEM_BUDGET - fixed) // slot_bytes))
    vmem, dma = pltpu.VMEM, pltpu.SemaphoreType.DMA
    flops = 4 * total_rows * width * own_units
    result = pl.pallas_call(
        functools.partial(kernel, sections, shards, slots),
        out_shape=jax.ShapeDtypeStruct((2 * sections, LANES), jnp.float32),
        in_specs=[pl.BlockSpec(memory_space=vmem)] * 5 + [pl.BlockSpec(memory_space=pl.ANY)] * 2,
        out_specs=pl.BlockSpec(memory_space=vmem),
        scratch_shapes=[
            vmem((CHUNKS, sections, 2, depth_z, 16, half), jnp.bfloat16),
            vmem((sections, 2, depth_z, 8, LANES), jnp.float32),
            vmem((slots, 2 * half, own_units), jnp.bfloat16),
            vmem((slots, 2 * half, own_units), jnp.bfloat16),
            vmem((total_rows, 2 * half), jnp.bfloat16),
            vmem((total_rows, own_units), jnp.float32),
            vmem((total_rows, own_units), jnp.float32),
            vmem((total_rows, LANES), jnp.float32),
            vmem((total_rows, 1), jnp.int32),
            vmem((total_rows, 1), jnp.int32),
            vmem((8, total_rows), jnp.float32),
            vmem((shards, 8, total_rows), jnp.float32),
            vmem((sections, 8, LANES), jnp.float32),
            vmem((sections, 8, LANES), jnp.float32),
            dma((slots, 2)),
            dma((CHUNKS + 1, line_kinds)),
            dma((CHUNKS + 1, line_kinds)),
            dma((CHUNKS + 1, depth_z)),
            dma((CHUNKS + 1, depth_z)),
            dma((shards,)),
            dma((shards,)),
            dma((sections,)),
            dma((sections,)),
        ],
        compiler_params=pltpu.CompilerParams(
            collective_id=0, has_side_effects=True, vmem_limit_bytes=VMEM_BUDGET + 3 * 2**20
        ),
        cost_estimate=pl.CostEstimate(
            flops=flops, bytes_accessed=4 * width * own_units, transcendentals=total_rows * own_units
        ),
    )(hidden, norm_gain, head_vector, pack_slot, owner_slot[None, :], gate_weight, up_weight)
    return pl.pallas_call(
        part_result,
        out_shape=(
            jax.ShapeDtypeStruct((1, total_rows // shards), jnp.float32),
            jax.ShapeDtypeStruct((sections, total_rows // (sections * shards)), jnp.float32),
        ),
        in_specs=[pl.BlockSpec(memory_space=vmem)],
        out_specs=(pl.BlockSpec(memory_space=vmem), pl.BlockSpec(memory_space=vmem)),
    )(result)


def solution(mesh):
    in_specs = (
        P(("section", "shard"), None),
        P("section", None),
        P("section", None, "shard"),
        P("section", None, "shard"),
        P("section", "shard"),
        P(),
        P(),
    )
    out_specs = (P("section", "shard"), P(None, ("section", "shard")))
    run = functools.partial(body, mesh.shape["section"], mesh.shape["shard"])
    return jax.shard_map(run, mesh=mesh, in_specs=in_specs, out_specs=out_specs, check_vma=False)
```

```python
import functools

import jax
import jax.numpy as jnp
from jax import lax
from jax.experimental import pallas as pl
from jax.experimental.pallas import tpu as pltpu
from jax.sharding import PartitionSpec as P

epsilon = 1e-06
MESH = pl.DeviceIdType.MESH
CHUNKS = 8
UNIT_TILE = 512
EARLY_SLOTS = 2
ROW_TILE = 256
LANES = 128
VMEM_BUDGET = 58 * 2**20


def kernel(
    sections, shards, slots,
    hidden_ref, gain_ref, head_ref, pack_ref, owner_ref, gate_ref, up_ref,
    result_ref,
    rows_buf, inv_buf, gate_ring, up_ring, normed, gate_acc, up_acc, part,
    pack_col, owner_col, message, partials, join_out, join_in,
    ring_sem, line_send, line_recv, z_send, z_recv, sum_send, sum_recv, join_send, join_recv,
):
    chunks, _, _, depth_z, _, half = rows_buf.shape
    width = 2 * half
    total_rows = pack_ref.shape[1]
    own_units = head_ref.shape[1]
    section_rows = total_rows // sections

    section = lax.axis_index("section")
    shard = lax.axis_index("shard")
    x, core = section // 2, section % 2
    z, y = shard // 2, shard % 2
    across_x = (section + 2) % sections
    across_core = 2 * x + 1 - core
    across_y = 1 - y
    shard_y = 2 * z + across_y

    def weight_copies(q):
        slot = q % slots
        rows = pl.ds(pl.multiple_of(q * width, width), width)
        return (
            pltpu.make_async_copy(gate_ref.at[0, rows, :], gate_ring.at[slot], ring_sem.at[slot, 0]),
            pltpu.make_async_copy(up_ref.at[0, rows, :], up_ring.at[slot], ring_sem.at[slot, 1]),
        )

    def load_weights(q):
        for copy in weight_copies(q):
            copy.start()

    barrier = pltpu.get_barrier_semaphore()
    for step in range(1, shards):
        pl.semaphore_signal(barrier, inc=1, device_id=(section, (shard + step) % shards), device_id_type=MESH)
    for step in range(1, sections):
        pl.semaphore_signal(barrier, inc=1, device_id=((section + step) % sections, shard), device_id_type=MESH)

    pl.loop(0, min(EARLY_SLOTS, slots))(load_weights)

    widened = hidden_ref[...].astype(jnp.float32)
    inv = lax.rsqrt(jnp.mean(widened * widened, axis=1, keepdims=True) + epsilon)
    inv_buf[section, y, z] = jnp.broadcast_to(inv, inv_buf.shape[3:])
    for q in range(chunks):
        low = widened[:, q * width : q * width + half]
        high = widened[:, q * width + half : (q + 1) * width]
        rows_buf[q, section, y, z] = jnp.concatenate([low, high], axis=0).astype(jnp.bfloat16)

    pl.semaphore_wait(barrier, shards - 1 + sections - 1)

    def line(q, sec, row):
        return inv_buf.at[sec, row] if q is None else rows_buf.at[q, sec, row]

    def plane(q, sec):
        return inv_buf.at[sec] if q is None else rows_buf.at[q, sec]

    def sem_row(q):
        return chunks if q is None else q

    def z_copy(q, step):
        block = inv_buf.at[section, y, z] if q is None else rows_buf.at[q, section, y, z]
        at = sem_row(q)
        return pltpu.make_async_remote_copy(
            src_ref=block, dst_ref=block,
            send_sem=z_send.at[at, step], recv_sem=z_recv.at[at, step],
            device_id=(section, 2 * ((z + step) % depth_z) + y), device_id_type=MESH,
        )

    def line_copy(q, kind):
        if kind == 0:
            source, target = line(q, section, y), (across_x, shard)
        elif kind == 1:
            source, target = line(q, section, y), (section, shard_y)
        elif kind == 2:
            odd = 0 if q is None else q % 2
            source = line(q, across_x + odd * (section - across_x), y + odd * (across_y - y))
            target = (section + odd * (across_x - section), shard_y + odd * (shard - shard_y))
        else:
            source = plane(q, section if kind == 3 else across_x)
            target = (across_core, shard)
        at = sem_row(q)
        return pltpu.make_async_remote_copy(
            src_ref=source, dst_ref=source,
            send_sem=line_send.at[at, kind], recv_sem=line_recv.at[at, kind],
            device_id=target, device_id_type=MESH,
        )

    def send_z(q):
        for step in range(1, depth_z):
            z_copy(q, step).start()

    def send_line(q):
        for step in range(1, depth_z):
            z_copy(q, step).wait_recv()
        for kind in (0, 1):
            line_copy(q, kind).start()

    def forward_line(q):
        line_copy(q, 0).wait_recv()
        line_copy(q, 1).wait_recv()
        for kind in (2, 3):
            line_copy(q, kind).start()

    def forward_diagonal(q):
        line_copy(q, 2).wait_recv()
        line_copy(q, 4).start()

    def collect(q):
        for kind in (3, 4):
            line_copy(q, kind).wait_recv()

    row_tiles = total_rows // ROW_TILE
    half_units = own_units // 2

    def normalise(q):
        for sec in range(sections):
            rows = slice(sec * section_rows, (sec + 1) * section_rows)
            inv_rows = inv_buf[sec].reshape(section_rows, LANES)
            for start in range(0, half, LANES):
                stacked = rows_buf[q, sec, :, :, :, start : start + LANES].astype(jnp.float32)
                for side in range(2):
                    at = side * half + start
                    columns = pl.ds(pl.multiple_of(q * width + at, LANES), LANES)
                    values = stacked[:, :, side * 8 : side * 8 + 8, :].reshape(section_rows, LANES)
                    scaled = values * inv_rows * gain_ref[:, columns]
                    normed[rows, at : at + LANES] = scaled.astype(jnp.bfloat16)

    def multiply(q, side):
        slot = q % slots

        def row_tile(rows):
            left = normed[rows, :]
            for start in range(side * half_units, (side + 1) * half_units, UNIT_TILE):
                columns = slice(start, start + UNIT_TILE)
                for ring, total in ((gate_ring, gate_acc), (up_ring, up_acc)):
                    total[rows, columns] += jnp.dot(
                        left, ring[slot, :, columns], preferred_element_type=jnp.float32
                    )

        if row_tiles == 1:
            row_tile(slice(0, ROW_TILE))
        else:
            pl.loop(0, row_tiles)(
                lambda index: row_tile(pl.ds(pl.multiple_of(index * ROW_TILE, ROW_TILE), ROW_TILE))
            )

    send_z(None)
    for q in range(3):
        send_z(q)

    @pl.loop(0, row_tiles)
    def _(index):
        rows = pl.ds(pl.multiple_of(index * ROW_TILE, ROW_TILE), ROW_TILE)
        gate_acc[rows, :] = jnp.zeros((ROW_TILE, own_units), jnp.float32)
        up_acc[rows, :] = jnp.zeros((ROW_TILE, own_units), jnp.float32)

    part[...] = jnp.zeros_like(part)

    send_line(None)
    send_line(0)
    pl.loop(3, chunks)(send_z)
    pl.loop(min(EARLY_SLOTS, slots), slots)(load_weights)
    forward_line(None)
    send_line(1)
    forward_line(0)

    sub = lax.broadcasted_iota(jnp.int32, (total_rows, total_rows), 0)
    lane = lax.broadcasted_iota(jnp.int32, (total_rows, total_rows), 1)
    in_section = sub % section_rows
    held_z, held_y = in_section // 8 % depth_z, in_section // (8 * depth_z)
    token = sub - in_section + (2 * held_z + held_y) * 8 + sub % 8
    pack_row = pack_ref[pl.ds(section, 1), :]
    pack_col[...] = jnp.sum(jnp.where(token == lane, pack_row, 0), axis=1, keepdims=True)
    owner_col[...] = jnp.sum(jnp.where(token == lane, owner_ref[...], 0), axis=1, keepdims=True)

    forward_diagonal(None)
    send_line(2)
    forward_line(1)
    forward_diagonal(0)
    collect(None)
    collect(0)

    @pl.loop(0, chunks)
    def _(q):
        for copy in weight_copies(q):
            copy.wait()
        normalise(q)
        multiply(q, 0)

        @pl.when(q + 3 < chunks)
        def _():
            send_line(q + 3)

        @pl.when(q + 2 < chunks)
        def _():
            forward_line(q + 2)

        @pl.when(q + 1 < chunks)
        def _():
            forward_diagonal(q + 1)

        multiply(q, 1)

        @pl.when(q + slots < chunks)
        def _():
            load_weights(q + slots)

        @pl.when(q + 1 < chunks)
        def _():
            collect(q + 1)

    @pl.loop(0, row_tiles * (own_units // LANES))
    def _(index):
        per_row = own_units // LANES
        rows = pl.ds(pl.multiple_of((index // per_row) * ROW_TILE, ROW_TILE), ROW_TILE)
        columns = pl.ds(pl.multiple_of((index % per_row) * LANES, LANES), LANES)
        gate = gate_acc[rows, columns]
        activated = gate / (1.0 + jnp.exp(-gate)) * up_acc[rows, columns]
        part[rows, :] += activated * head_ref[:, columns].astype(jnp.float32)

    own_col = jnp.sum(part[...], axis=1, keepdims=True)
    own_row = jnp.sum(jnp.where(sub == lane, own_col, 0.0), axis=0, keepdims=True)
    message[...] = jnp.broadcast_to(own_row, message.shape)
    partials[shard] = message[...]

    def sum_copy(step):
        return pltpu.make_async_remote_copy(
            src_ref=message, dst_ref=partials.at[shard],
            send_sem=sum_send.at[step], recv_sem=sum_recv.at[step],
            device_id=(section, (shard + step) % shards), device_id_type=MESH,
        )

    for step in range(1, shards):
        sum_copy(step).start()

    def finish_sends(q):
        for step in range(1, depth_z):
            z_copy(q, step).wait_send()
        for kind in range(5):
            line_copy(q, kind).wait_send()

    finish_sends(None)
    pl.loop(0, chunks)(finish_sends)

    for step in range(1, shards):
        sum_copy(step).wait_recv()
    scores = partials[0]
    for other in range(1, shards):
        scores = scores + partials[other]
    scores = scores[:1, :]
    flipped = section % 2 == 1
    log_sigmoid = jnp.minimum(scores, 0.0) - jnp.log1p(jnp.exp(-jnp.abs(scores)))
    values = jnp.where(flipped, log_sigmoid, scores)
    value_col = jnp.sum(jnp.where(sub == lane, values, 0.0), axis=1, keepdims=True)

    lanes = lax.broadcasted_iota(jnp.int32, (total_rows, LANES), 1)
    own_count = total_rows // (sections * shards)
    pack_rows = total_rows // shards

    def owned_by(sec):
        base = (sec * shards + shard) * own_count
        return jnp.sum(jnp.where(owner_col[...] == base + lanes, value_col, 0.0), axis=0, keepdims=True)

    def join_copy(step):
        return pltpu.make_async_remote_copy(
            src_ref=join_out.at[step], dst_ref=join_in.at[section],
            send_sem=join_send.at[step], recv_sem=join_recv.at[step],
            device_id=((section + step) % sections, shard), device_id_type=MESH,
        )

    for step in range(1, sections):
        join_out[step] = jnp.broadcast_to(owned_by((section + step) % sections), join_out.shape[1:])
        join_copy(step).start()
    join_in[section] = jnp.broadcast_to(owned_by(section), join_in.shape[1:])

    base = shard * pack_rows
    packed = jnp.sum(jnp.where(pack_col[...] == base + lanes, value_col, 0.0), axis=0, keepdims=True)
    result_ref[sections:, :] = jnp.broadcast_to(packed, (result_ref.shape[0] - sections, LANES))

    for step in range(1, sections):
        join_copy(step).wait_recv()
    for sec in range(sections):
        result_ref[sec : sec + 1, :] = join_in[sec][:1, :]

    for step in range(1, shards):
        sum_copy(step).wait_send()
    for step in range(1, sections):
        join_copy(step).wait_send()


def part_result(result_ref, scores_ref, joined_ref):
    sections = joined_ref.shape[0]
    scores_ref[...] = result_ref[sections : sections + 1, : scores_ref.shape[1]]
    joined_ref[...] = result_ref[:sections, : joined_ref.shape[1]]


def body(sections, shards, hidden, norm_gain, gate_weight, up_weight, head_vector, pack_slot, owner_slot):
    total_rows = owner_slot.shape[0]
    width = hidden.shape[1]
    own_units = head_vector.shape[1]
    half = width // CHUNKS // 2
    depth_z = shards // 2
    line_kinds = 5
    fixed = total_rows * (width * 2 + own_units * 8 + 2 * half * 2 + LANES * 4 * 4)
    fixed += shards * total_rows * 32 + 4 * 2**20
    slot_bytes = 2 * (width // CHUNKS) * own_units * 2
    slots = max(1, min(CHUNKS, (VMEM_BUDGET - fixed) // slot_bytes))
    vmem, dma = pltpu.VMEM, pltpu.SemaphoreType.DMA
    flops = 4 * total_rows * width * own_units
    result = pl.pallas_call(
        functools.partial(kernel, sections, shards, slots),
        out_shape=jax.ShapeDtypeStruct((2 * sections, LANES), jnp.float32),
        in_specs=[pl.BlockSpec(memory_space=vmem)] * 5 + [pl.BlockSpec(memory_space=pl.ANY)] * 2,
        out_specs=pl.BlockSpec(memory_space=vmem),
        scratch_shapes=[
            vmem((CHUNKS, sections, 2, depth_z, 16, half), jnp.bfloat16),
            vmem((sections, 2, depth_z, 8, LANES), jnp.float32),
            vmem((slots, 2 * half, own_units), jnp.bfloat16),
            vmem((slots, 2 * half, own_units), jnp.bfloat16),
            vmem((total_rows, 2 * half), jnp.bfloat16),
            vmem((total_rows, own_units), jnp.float32),
            vmem((total_rows, own_units), jnp.float32),
            vmem((total_rows, LANES), jnp.float32),
            vmem((total_rows, 1), jnp.int32),
            vmem((total_rows, 1), jnp.int32),
            vmem((8, total_rows), jnp.float32),
            vmem((shards, 8, total_rows), jnp.float32),
            vmem((sections, 8, LANES), jnp.float32),
            vmem((sections, 8, LANES), jnp.float32),
            dma((slots, 2)),
            dma((CHUNKS + 1, line_kinds)),
            dma((CHUNKS + 1, line_kinds)),
            dma((CHUNKS + 1, depth_z)),
            dma((CHUNKS + 1, depth_z)),
            dma((shards,)),
            dma((shards,)),
            dma((sections,)),
            dma((sections,)),
        ],
        compiler_params=pltpu.CompilerParams(
            collective_id=0, has_side_effects=True, vmem_limit_bytes=VMEM_BUDGET + 3 * 2**20
        ),
        cost_estimate=pl.CostEstimate(
            flops=flops, bytes_accessed=4 * width * own_units, transcendentals=total_rows * own_units
        ),
    )(hidden, norm_gain, head_vector, pack_slot, owner_slot[None, :], gate_weight, up_weight)
    return pl.pallas_call(
        part_result,
        out_shape=(
            jax.ShapeDtypeStruct((1, total_rows // shards), jnp.float32),
            jax.ShapeDtypeStruct((sections, total_rows // (sections * shards)), jnp.float32),
        ),
        in_specs=[pl.BlockSpec(memory_space=vmem)],
        out_specs=(pl.BlockSpec(memory_space=vmem), pl.BlockSpec(memory_space=vmem)),
    )(result)


def solution(mesh):
    in_specs = (
        P(("section", "shard"), None),
        P("section", None),
        P("section", None, "shard"),
        P("section", None, "shard"),
        P("section", "shard"),
        P(),
        P(),
    )
    out_specs = (P("section", "shard"), P(None, ("section", "shard")))
    run = functools.partial(body, mesh.shape["section"], mesh.shape["shard"])
    return jax.shard_map(run, mesh=mesh, in_specs=in_specs, out_specs=out_specs, check_vma=False)
```
